32 devices in a mesh: row: 4 (over y, x), seq: 8 (over z, core).
Axes of the slice: x: 2, y: 2, z: 4, core: 2. Of those that a mesh axis runs over, the one named last changes fastest.
Arguments:
- tokens: bfloat16 [16, 1024, 512], P('row', 'seq'), may hold values from -6 to 6
- w_query: float32 [512, 512], P(('row', 'seq')), may hold values from -0.25 to 0.25
- w_key: float32 [512, 512], P(('row', 'seq')), may hold values from -0.25 to 0.25
- w_value: float32 [512, 512], P(('row', 'seq')), may hold values from -0.25 to 0.25
- w_gate: float32 [512, 8], P(('row', 'seq')), may hold values from -0.25 to 0.25
- w_out: float32 [512, 512], P(('row', 'seq')), may hold values from -0.75 to 0.75
- w_up: float32 [512, 2048], P(('row', 'seq')), may hold values from -0.25 to 0.25
- w_down: float32 [2048, 512], P(('row', 'seq')), may hold values from -0.125 to 0.125
- gain_one: float32 [512], P(('row', 'seq')), may hold values from 0.5 to 1.5
- shift_one: float32 [512], P(('row', 'seq')), may hold values from -3 to 3
- gain_two: float32 [512], P(('row', 'seq')), may hold values from 0.5 to 1.5
- shift_two: float32 [512], P(('row', 'seq')), may hold values from -3 to 3
- bias_up: float32 [2048], P(('row', 'seq')), may hold values from -3 to 3
- bias_down: float32 [512], P(('row', 'seq')), may hold values from -3 to 3
- gate_bias: float32 [8], replicated, may hold values from 2 to 14
- start_state: float32 [16, 8, 256, 64], P('row'), may hold values from -6 to 6
- start_norm: float32 [16, 8, 256], P('row'), may hold values from 0.03 to 0.3
- rand_feat: float32 [8, 256, 64], replicated, may hold values from -6 to 6
- out_grad: bfloat16 [16, 1024, 512], P('row', 'seq'), may hold values from -6 to 6
- state_grad: float32 [16, 8, 256, 64], P('row', None, 'seq'), may hold values from -6 to 6
- norm_grad: float32 [16, 8, 256], P('row', None, 'seq'), may hold values from -6 to 6
Outputs:
- result: bfloat16 [16, 1024, 512], P('row', 'seq')
- final_state: float32 [16, 8, 256, 64], P('row', None, 'seq')
- final_norm: float32 [16, 8, 256], P('row', None, 'seq')
- input_grad: bfloat16 [16, 1024, 512], P('row', 'seq')
- start_state_grad: float32 [16, 8, 256, 64], P('row', None, 'seq')
- start_norm_grad: float32 [16, 8, 256], P('row', None, 'seq')
- grad_query: float32 [512, 512], P(('row', 'seq'))
- grad_key: float32 [512, 512], P(('row', 'seq'))
- grad_value: float32 [512, 512], P(('row', 'seq'))
- grad_gate: float32 [512, 8], P(('row', 'seq'))
- grad_out: float32 [512, 512], P(('row', 'seq'))
- grad_up: float32 [512, 2048], P(('row', 'seq'))
- grad_down: float32 [2048, 512], P(('row', 'seq'))
- grad_gain_one: float32 [512], P(('row', 'seq'))
- grad_shift_one: float32 [512], P(('row', 'seq'))
- grad_gain_two: float32 [512], P(('row', 'seq'))
- grad_shift_two: float32 [512], P(('row', 'seq'))
- grad_bias_up: float32 [2048], P(('row', 'seq'))
- grad_bias_down: float32 [512], P(('row', 'seq'))
- grad_gate_bias: float32 [8], replicated
The draws below stay inside these ranges and needn't reach their ends.
All inputs are finite; a program needn't handle non-finite values.
Results may differ from the reference program's by a relative error of at most 0.0075.
The reference program's roundings to bfloat16 on the way count: a program that leaves them out, or rounds other values in their place, can miss the bound.
Values may be sent and summed in bfloat16 or wider, within the bound.
A program may use at most 832 MiB of HBM per device.

```python
import math
import jax
import jax.numpy as jnp
from jax import lax

D = 512
HEADS = 8
HEAD_DIM = 64
FEAT = 256
FF = 2048
SPAN = 128
BATCH = 16
LENGTH = 1024


def draw_gate_bias(key, part):
    key = jax.random.fold_in(key, 7)
    pick_key, jitter_key = jax.random.split(key)
    chooser = jax.random.uniform(pick_key, (HEADS,), jnp.float32)
    slow_share = 0.5
    slow_value = jnp.log(jnp.float32(LENGTH)) + 0.5
    jitter = jnp.clip(jax.random.normal(jitter_key, (HEADS,), jnp.float32), -1.0, 1.0)
    return jnp.where(chooser < slow_share, slow_value, 3.5) + 0.3 * jitter


def block_levels(stream_key, extent, shards, least, largest):
    loudness = 1.0
    for axis_at, blocks in shards:
        draws = jax.random.uniform(jax.random.fold_in(jax.random.fold_in(stream_key, 6), axis_at), (blocks,), jnp.float32, least / len(shards), largest / len(shards))
        loudness = loudness * jnp.repeat(jnp.exp(draws), extent[axis_at] // blocks).reshape((-1,) + (1,) * (len(extent) - 1 - axis_at))
    return loudness


def normal_values(key, dims, scale, bound, cuts=(), held_as=jnp.bfloat16):
    loudness = block_levels(key, dims, cuts, -0.22, 0.18) if cuts else 1.0
    values = jax.random.normal(key, dims, jnp.float32) * scale * loudness
    return jnp.minimum(jnp.maximum(values, -bound), bound).astype(held_as)


def setup_inputs(seed: int = 0) -> dict:
    key_list = jax.random.split(jax.random.key(seed), 22)
    tokens = normal_values(key_list[0], (BATCH, LENGTH, D), 1.0, 6.0, ((0, 4), (1, 8)))
    w_query = normal_values(key_list[1], (D, D), D ** -0.5, 0.25, ((0, 32),), jnp.float32)
    w_key = normal_values(key_list[2], (D, D), D ** -0.5, 0.25, ((0, 32),), jnp.float32)
    w_value = normal_values(key_list[3], (D, D), D ** -0.5, 0.25, ((0, 32),), jnp.float32)
    w_gate = normal_values(key_list[4], (D, HEADS), D ** -0.5, 0.25, ((0, 32),), jnp.float32)
    w_out = normal_values(key_list[5], (D, D), (D // 8) ** -0.5, 0.75, ((0, 32),), jnp.float32)
    w_up = normal_values(key_list[6], (D, FF), D ** -0.5, 0.25, ((0, 32),), jnp.float32)
    w_down = normal_values(key_list[7], (FF, D), FF ** -0.5, 0.125, ((0, 32),), jnp.float32)
    gain_one = jnp.clip(1.0 + 0.1 * jax.random.normal(key_list[8], (D,), jnp.float32), 0.5, 1.5)
    shift_one = normal_values(key_list[9], (D,), 0.3, 3.0, ((0, 32),), jnp.float32)
    gain_two = jnp.clip(1.0 + 0.1 * jax.random.normal(key_list[10], (D,), jnp.float32), 0.5, 1.5)
    shift_two = normal_values(key_list[11], (D,), 0.3, 3.0, ((0, 32),), jnp.float32)
    bias_up = normal_values(key_list[12], (FF,), 0.3, 3.0, ((0, 32),), jnp.float32)
    bias_down = normal_values(key_list[13], (D,), 0.3, 3.0, ((0, 32),), jnp.float32)
    gate_bias = draw_gate_bias(jax.random.fold_in(key_list[21], 71), 0)
    start_state = normal_values(key_list[15], (BATCH, HEADS, FEAT, HEAD_DIM), 1.0, 6.0, ((0, 4),), jnp.float32)
    start_norm = jnp.clip(jnp.exp(math.log(0.3) - 2.3025852 * jax.random.uniform(key_list[16], (BATCH, HEADS, FEAT), jnp.float32) ** block_levels(key_list[16], (BATCH, HEADS, FEAT), ((0, 4),), -0.2, 0.2)), 0.03, 0.3)
    rand_feat = normal_values(key_list[17], (HEADS, FEAT, HEAD_DIM), 1.0, 6.0, (), jnp.float32)
    out_grad = normal_values(key_list[18], (BATCH, LENGTH, D), 1.0, 6.0, ((0, 4), (1, 8)))
    state_grad = normal_values(key_list[19], (BATCH, HEADS, FEAT, HEAD_DIM), 1.0, 6.0, ((0, 4), (2, 8)), jnp.float32)
    norm_grad = normal_values(key_list[20], (BATCH, HEADS, FEAT), 1.0, 6.0, ((0, 4), (2, 8)), jnp.float32)
    return {"tokens": tokens, "w_query": w_query, "w_key": w_key, "w_value": w_value, "w_gate": w_gate, "w_out": w_out, "w_up": w_up, "w_down": w_down, "gain_one": gain_one, "shift_one": shift_one, "gain_two": gain_two, "shift_two": shift_two, "bias_up": bias_up, "bias_down": bias_down, "gate_bias": gate_bias, "start_state": start_state, "start_norm": start_norm, "rand_feat": rand_feat, "out_grad": out_grad, "state_grad": state_grad, "norm_grad": norm_grad}


finest = lax.Precision.HIGHEST

@jax.custom_vjp
def low(v):
    return lax.optimization_barrier(v.astype(jnp.bfloat16)).astype(jnp.float32)

@jax.custom_vjp
def low_back(v):
    return v

def low_keep(v):
    return (low(v), None)

def low_pass(kept, grad):
    return (grad,)

def back_keep(v):
    return (v, None)

def back_low(kept, grad):
    return (low(grad),)
low.defvjp(low_keep, low_pass)
low_back.defvjp(back_keep, back_low)

def normed(values, gain, shift):
    centre = lax.optimization_barrier(jnp.mean(values, axis=-1, keepdims=True))
    centred = values - centre
    spread = lax.optimization_barrier(jnp.mean(centred * centred, axis=-1, keepdims=True))
    return centred * lax.rsqrt(spread + 1e-05) * gain + shift

def features(vectors, rand_feat):
    unit = vectors * lax.rsqrt(lax.optimization_barrier(jnp.sum(vectors * vectors, axis=-1, keepdims=True)) + 1e-06)
    mapped = jnp.einsum('sthe,hfe->sthf', unit, rand_feat, precision=finest)
    return jnp.exp(mapped - 0.5) / math.sqrt(rand_feat.shape[1])

def intra(projected, gate_bias, rand_feat):
    heads, feat, head_dim = rand_feat.shape
    seq_count, block_len, _ = projected.shape
    model_width = heads * head_dim
    query = projected[..., :model_width].reshape(seq_count, block_len, heads, head_dim)
    key_vec = projected[..., model_width:2 * model_width].reshape(seq_count, block_len, heads, head_dim)
    value = projected[..., 2 * model_width:3 * model_width].reshape(seq_count, block_len, heads, head_dim)
    logit = projected[..., 3 * model_width:] + gate_bias
    log_keep = -jax.nn.softplus(-logit)
    write = jax.nn.sigmoid(-logit)
    cumul = jnp.cumsum(log_keep, axis=1)
    q_feat = features(query, rand_feat)
    k_feat = features(key_vec, rand_feat)
    by_head = jnp.transpose(cumul, (0, 2, 1))
    differ = by_head[:, :, :, None] - by_head[:, :, None, :]
    lower = jnp.arange(block_len)[:, None] >= jnp.arange(block_len)[None, :]
    decay = jnp.where(lower, jnp.exp(jnp.where(lower, differ, 0.0)), 0.0)
    decay = decay * jnp.transpose(write, (0, 2, 1))[:, :, None, :]
    scores = jnp.einsum('sthf,suhf->shtu', q_feat, k_feat, precision=finest) * decay
    numer = jnp.einsum('shtu,suhe->sthe', scores, value, precision=finest)
    denom = jnp.transpose(lax.optimization_barrier(jnp.sum(scores, axis=-1)), (0, 2, 1))
    ending = cumul[:, -1, :]
    weighted = k_feat * (jnp.exp(ending[:, None, :] - cumul) * write)[..., None]
    local_state = jnp.einsum('suhf,suhe->shfe', weighted, value, precision=finest)
    local_norm = lax.optimization_barrier(jnp.sum(weighted, axis=1))
    return (numer, denom, cumul, q_feat, ending, local_state, local_norm)

def inter(numer, denom, cumul, q_feat, state, norm):
    growth = jnp.exp(cumul)
    full_num = numer + growth[..., None] * jnp.einsum('sthf,shfe->sthe', q_feat, state, precision=finest)
    full_den = denom + growth * jnp.einsum('sthf,shf->sth', q_feat, norm, precision=finest)
    merged = full_num / full_den[..., None]
    return merged.reshape(merged.shape[0], merged.shape[1], -1)

def mixer(projected, gate_bias, rand_feat, state, norm):
    numer, denom, cumul, q_feat, ending, local_state, local_norm = intra(projected, gate_bias, rand_feat)
    output = inter(numer, denom, cumul, q_feat, state, norm)
    carry = jnp.exp(ending)
    return (output, carry[:, :, None, None] * state + local_state, carry[:, :, None] * norm + local_norm)

def project(left, right):
    return jnp.einsum('btd,df->btf', left, right, precision=finest)

def forward(rand_feat, tokens, w_query, w_key, w_value, w_gate, w_out, w_up, w_down, gain_one, shift_one, gain_two, shift_two, bias_up, bias_down, gate_bias, start_state, start_norm):
    first = low(normed(tokens, low(gain_one), low(shift_one)))
    joined = jnp.concatenate([low(w_query), low(w_key), low(w_value), low(w_gate)], axis=1)
    projected = low_back(project(first, joined))
    batch_count, seq_len, columns = projected.shape
    blocks = projected.reshape(batch_count, seq_len // SPAN, SPAN, columns).transpose(1, 0, 2, 3)

    def advance(carry, piece):
        output, state, norm = mixer(piece, gate_bias, rand_feat, carry[0], carry[1])
        return ((state, norm), output)
    (last_state, last_norm), outputs = lax.scan(jax.checkpoint(advance), (start_state, start_norm), blocks)
    attended = low(outputs.transpose(1, 0, 2, 3).reshape(batch_count, seq_len, -1))
    mixed = tokens + low_back(project(attended, low(w_out)))
    second = low(normed(mixed, low(gain_two), low(shift_two)))
    hidden = low(jax.nn.gelu(low_back(project(second, low(w_up)) + low(bias_up))))
    result = mixed + low_back(project(hidden, low(w_down))) + low(bias_down)
    return (result, last_state, last_norm)

def reference(tokens, w_query, w_key, w_value, w_gate, w_out, w_up, w_down, gain_one, shift_one, gain_two, shift_two, bias_up, bias_down, gate_bias, start_state, start_norm, rand_feat, out_grad, state_grad, norm_grad):
    primal, pullback = jax.vjp(lambda *inputs: forward(rand_feat, *inputs), tokens.astype(jnp.float32), w_query, w_key, w_value, w_gate, w_out, w_up, w_down, gain_one, shift_one, gain_two, shift_two, bias_up, bias_down, gate_bias, start_state, start_norm)
    grads = pullback((out_grad.astype(jnp.float32), state_grad, norm_grad))
    return (primal[0].astype(jnp.bfloat16), primal[1], primal[2], grads[0].astype(jnp.bfloat16), grads[15], grads[16], grads[1], grads[2], grads[3], grads[4], grads[5], grads[6], grads[7], grads[8], grads[9], grads[10], grads[11], grads[12], grads[13], grads[14])
```

```python
import math

import jax
import jax.numpy as jnp
from jax import lax
from jax.sharding import PartitionSpec as P

finest = lax.Precision.HIGHEST


def swap_out(part):
    count = lax.axis_size("seq")
    shape = part.shape
    cut = part.reshape(shape[:2] + (count, shape[2] // count) + shape[3:])
    return lax.all_to_all(jnp.moveaxis(cut, 2, 0), "seq", 0, 0)


def swap_back(part):
    whole = jnp.moveaxis(lax.all_to_all(part, "seq", 0, 0), 0, 2)
    shape = whole.shape
    return whole.reshape(shape[:2] + (shape[2] * shape[3],) + shape[4:])


def chain(first, factors, pieces, reverse):
    def step(total, block):
        factor, piece = block
        spread = factor.reshape(factor.shape + (1,) * (piece.ndim - factor.ndim))
        return spread * total + piece, total

    return lax.scan(step, first, (factors, pieces), reverse=reverse)


def normed(values, gain, shift):
    centre = jnp.mean(values, axis=-1, keepdims=True)
    centred = values - centre
    spread = jnp.mean(centred * centred, axis=-1, keepdims=True)
    return centred * lax.rsqrt(spread + 1e-05) * gain + shift


def features(vectors, rand_feat):
    unit = vectors * lax.rsqrt(jnp.sum(vectors * vectors, axis=-1, keepdims=True) + 1e-06)
    mapped = jnp.einsum("sthe,hfe->sthf", unit, rand_feat, precision=finest)
    return jnp.exp(mapped - 0.5) / math.sqrt(rand_feat.shape[1])


def intra(projected, gate_bias, rand_feat):
    heads, feat, head_dim = rand_feat.shape
    seq_count, block_len, _ = projected.shape
    model_width = heads * head_dim
    query = projected[..., :model_width].reshape(seq_count, block_len, heads, head_dim)
    key_vec = projected[..., model_width : 2 * model_width].reshape(
        seq_count, block_len, heads, head_dim
    )
    value = projected[..., 2 * model_width : 3 * model_width].reshape(
        seq_count, block_len, heads, head_dim
    )
    logit = projected[..., 3 * model_width :] + gate_bias
    log_keep = -jax.nn.softplus(-logit)
    write = jax.nn.sigmoid(-logit)
    cumul = jnp.cumsum(log_keep, axis=1)
    q_feat = features(query, rand_feat)
    k_feat = features(key_vec, rand_feat)
    by_head = jnp.transpose(cumul, (0, 2, 1))
    differ = by_head[:, :, :, None] - by_head[:, :, None, :]
    lower = jnp.arange(block_len)[:, None] >= jnp.arange(block_len)[None, :]
    decay = jnp.where(lower, jnp.exp(jnp.where(lower, differ, 0.0)), 0.0)
    decay = decay * jnp.transpose(write, (0, 2, 1))[:, :, None, :]
    scores = jnp.einsum("sthf,suhf->shtu", q_feat, k_feat, precision=finest) * decay
    numer = jnp.einsum("shtu,suhe->sthe", scores, value, precision=finest)
    denom = jnp.transpose(jnp.sum(scores, axis=-1), (0, 2, 1))
    ending = cumul[:, -1, :]
    weighted = k_feat * (jnp.exp(ending[:, None, :] - cumul) * write)[..., None]
    local_state = jnp.einsum("suhf,suhe->shfe", weighted, value, precision=finest)
    local_norm = jnp.sum(weighted, axis=1)
    return (numer, denom, cumul, q_feat, ending, local_state, local_norm)


def inter(numer, denom, cumul, q_feat, state, norm):
    growth = jnp.exp(cumul)
    full_num = numer + growth[..., None] * jnp.einsum(
        "sthf,shfe->sthe", q_feat, state, precision=finest
    )
    full_den = denom + growth * jnp.einsum("sthf,shf->sth", q_feat, norm, precision=finest)
    merged = full_num / full_den[..., None]
    return merged.reshape(merged.shape[0], merged.shape[1], -1)


def mixer(projected, gate_bias, rand_feat, state, norm):
    numer, denom, cumul, q_feat, ending, local_state, local_norm = intra(
        projected, gate_bias, rand_feat
    )
    output = inter(numer, denom, cumul, q_feat, state, norm)
    carry = jnp.exp(ending)
    return (
        output,
        carry[:, :, None, None] * state + local_state,
        carry[:, :, None] * norm + local_norm,
    )


def matmul(left, right):
    return jnp.dot(left, right, preferred_element_type=jnp.float32)


def left_inner(left, right):
    return lax.dot_general(
        left, right, (((0,), (0,)), ((), ())), preferred_element_type=jnp.float32
    )


def right_inner(left, right):
    return lax.dot_general(
        left, right, (((1,), (1,)), ((), ())), preferred_element_type=jnp.float32
    )


def body(
    tokens,
    w_query,
    w_key,
    w_value,
    w_gate,
    w_out,
    w_up,
    w_down,
    gain_one,
    shift_one,
    gain_two,
    shift_two,
    bias_up,
    bias_down,
    gate_bias,
    start_state,
    start_norm,
    rand_feat,
    out_grad,
    state_grad,
    norm_grad,
):
    bf = jnp.bfloat16
    gathered = (
        lax.all_gather(w_query.astype(bf), ("row", "seq"), axis=0, tiled=True),
        lax.all_gather(w_key.astype(bf), ("row", "seq"), axis=0, tiled=True),
        lax.all_gather(w_value.astype(bf), ("row", "seq"), axis=0, tiled=True),
        lax.all_gather(w_gate.astype(bf), ("row", "seq"), axis=0, tiled=True),
        lax.all_gather(w_out.astype(bf), ("row", "seq"), axis=0, tiled=True),
        lax.all_gather(w_up.astype(bf), ("row", "seq"), axis=0, tiled=True),
        lax.all_gather(w_down.astype(bf), ("row", "seq"), axis=0, tiled=True),
        lax.all_gather(gain_one.astype(bf), ("row", "seq"), axis=0, tiled=True),
        lax.all_gather(shift_one.astype(bf), ("row", "seq"), axis=0, tiled=True),
        lax.all_gather(gain_two.astype(bf), ("row", "seq"), axis=0, tiled=True),
        lax.all_gather(shift_two.astype(bf), ("row", "seq"), axis=0, tiled=True),
        lax.all_gather(bias_up.astype(bf), ("row", "seq"), axis=0, tiled=True),
        lax.all_gather(bias_down.astype(bf), ("row", "seq"), axis=0, tiled=True),
    )
    (
        query_half,
        key_half,
        value_half,
        gate_half,
        out_half,
        up_half,
        down_half,
        gain_first,
        shift_first,
        gain_second,
        shift_second,
        up_bias,
        down_bias,
    ) = gathered
    gain_first = gain_first.astype(jnp.float32)
    shift_first = shift_first.astype(jnp.float32)
    gain_second = gain_second.astype(jnp.float32)
    shift_second = shift_second.astype(jnp.float32)
    local_seqs, block_len, model_width = tokens.shape
    row_total = local_seqs * block_len
    token_rows = tokens.reshape(row_total, model_width).astype(jnp.float32)
    first_half = normed(token_rows, gain_first, shift_first).astype(bf)
    input_weight = jnp.concatenate([query_half, key_half, value_half, gate_half], axis=1)
    proj_blocks = matmul(first_half, input_weight).reshape(local_seqs, block_len, -1)
    numer, denom, cumul, q_feat, ending, local_state, local_norm = intra(
        proj_blocks, gate_bias, rand_feat
    )
    factors = jnp.exp(lax.all_gather(ending, "seq"))
    slice_len = state_grad.shape[2]
    offset = lax.axis_index("seq") * slice_len
    state_slice = lax.dynamic_slice_in_dim(start_state, offset, slice_len, 2)
    norm_slice = lax.dynamic_slice_in_dim(start_norm, offset, slice_len, 2)
    final_state, states = chain(state_slice, factors, swap_out(local_state), False)
    final_norm, norms = chain(norm_slice, factors, swap_out(local_norm), False)
    state_in = swap_back(states)
    norm_in = swap_back(norms)
    attended = inter(numer, denom, cumul, q_feat, state_in, norm_in)
    attended_half = attended.reshape(row_total, model_width).astype(bf)
    mixed = token_rows + matmul(attended_half, out_half)
    second_half = normed(mixed, gain_second, shift_second).astype(bf)
    pre_act = matmul(second_half, up_half) + up_bias.astype(jnp.float32)
    hidden_half = jax.nn.gelu(pre_act).astype(bf)
    result = mixed + matmul(hidden_half, down_half) + down_bias.astype(jnp.float32)
    grad_rows = out_grad.reshape(row_total, model_width)
    grad_float = grad_rows.astype(jnp.float32)
    grad_bias_down = jnp.sum(grad_float, axis=0)
    grad_down = left_inner(hidden_half, grad_rows)
    grad_hidden = right_inner(grad_rows, down_half)
    _, gelu_back = jax.vjp(jax.nn.gelu, pre_act)
    grad_pre_half = gelu_back(grad_hidden)[0].astype(bf)
    grad_bias_up = jnp.sum(grad_pre_half.astype(jnp.float32), axis=0)
    grad_up = left_inner(second_half, grad_pre_half)
    grad_second = right_inner(grad_pre_half, up_half)
    _, second_back = jax.vjp(normed, mixed, gain_second, shift_second)
    mixed_from_norm, grad_gain_two, grad_shift_two = second_back(grad_second)
    grad_mixed = grad_float + mixed_from_norm
    grad_mixed_half = grad_mixed.astype(bf)
    grad_out = left_inner(attended_half, grad_mixed_half)
    grad_att = right_inner(grad_mixed_half, out_half).reshape(local_seqs, block_len, model_width)
    _, inter_back = jax.vjp(
        lambda state, norm: inter(numer, denom, cumul, q_feat, state, norm), state_in, norm_in
    )
    own_state_grad, own_norm_grad = inter_back(grad_att)
    start_state_grad, state_carries = chain(state_grad, factors, swap_out(own_state_grad), True)
    start_norm_grad, norm_carries = chain(norm_grad, factors, swap_out(own_norm_grad), True)
    carry_state = swap_back(state_carries)
    carry_norm = swap_back(norm_carries)

    def mixer_local(proj_part, bias_part):
        return mixer(proj_part, bias_part, rand_feat, state_in, norm_in)

    _, mixer_back = jax.vjp(mixer_local, proj_blocks, gate_bias)
    grad_proj, grad_bias_gate = mixer_back((grad_att, carry_state, carry_norm))
    grad_proj_half = grad_proj.reshape(row_total, -1).astype(bf)
    grad_joined = left_inner(first_half, grad_proj_half)
    grad_first = right_inner(grad_proj_half, input_weight)
    _, first_back = jax.vjp(normed, token_rows, gain_first, shift_first)
    tokens_from_norm, grad_gain_one, grad_shift_one = first_back(grad_first)
    input_grad = (grad_mixed + tokens_from_norm).astype(bf).reshape(tokens.shape)
    grad_query = grad_joined[:, :model_width]
    grad_key = grad_joined[:, model_width : 2 * model_width]
    grad_value = grad_joined[:, 2 * model_width : 3 * model_width]
    grad_gate = grad_joined[:, 3 * model_width :]
    owned = (
        lax.psum_scatter(grad_query, ("row", "seq"), scatter_dimension=0, tiled=True),
        lax.psum_scatter(grad_key, ("row", "seq"), scatter_dimension=0, tiled=True),
        lax.psum_scatter(grad_value, ("row", "seq"), scatter_dimension=0, tiled=True),
        lax.psum_scatter(grad_gate, ("row", "seq"), scatter_dimension=0, tiled=True),
        lax.psum_scatter(grad_out, ("row", "seq"), scatter_dimension=0, tiled=True),
        lax.psum_scatter(grad_up, ("row", "seq"), scatter_dimension=0, tiled=True),
        lax.psum_scatter(grad_down, ("row", "seq"), scatter_dimension=0, tiled=True),
        lax.psum_scatter(grad_gain_one, ("row", "seq"), scatter_dimension=0, tiled=True),
        lax.psum_scatter(grad_shift_one, ("row", "seq"), scatter_dimension=0, tiled=True),
        lax.psum_scatter(grad_gain_two, ("row", "seq"), scatter_dimension=0, tiled=True),
        lax.psum_scatter(grad_shift_two, ("row", "seq"), scatter_dimension=0, tiled=True),
        lax.psum_scatter(grad_bias_up, ("row", "seq"), scatter_dimension=0, tiled=True),
        lax.psum_scatter(grad_bias_down, ("row", "seq"), scatter_dimension=0, tiled=True),
    )
    gate_total = lax.psum(grad_bias_gate, ("row", "seq"))
    return (
        result.astype(bf).reshape(tokens.shape),
        final_state,
        final_norm,
        input_grad,
        start_state_grad,
        start_norm_grad,
        owned[0],
        owned[1],
        owned[2],
        owned[3],
        owned[4],
        owned[5],
        owned[6],
        owned[7],
        owned[8],
        owned[9],
        owned[10],
        owned[11],
        owned[12],
        gate_total,
    )


def solution(mesh):
    placed = (
        P("row", "seq", None),
        P(("row", "seq"), None),
        P(("row", "seq"), None),
        P(("row", "seq"), None),
        P(("row", "seq"), None),
        P(("row", "seq"), None),
        P(("row", "seq"), None),
        P(("row", "seq"), None),
        P(("row", "seq")),
        P(("row", "seq")),
        P(("row", "seq")),
        P(("row", "seq")),
        P(("row", "seq")),
        P(("row", "seq")),
        P(),
        P("row", None, None, None),
        P("row", None, None),
        P(),
        P("row", "seq", None),
        P("row", None, "seq", None),
        P("row", None, "seq"),
    )
    return jax.shard_map(
        body,
        mesh=mesh,
        in_specs=placed,
        out_specs=(
            P("row", "seq", None),
            P("row", None, "seq", None),
            P("row", None, "seq"),
            P("row", "seq", None),
            P("row", None, "seq", None),
            P("row", None, "seq"),
            P(("row", "seq"), None),
            P(("row", "seq"), None),
            P(("row", "seq"), None),
            P(("row", "seq"), None),
            P(("row", "seq"), None),
            P(("row", "seq"), None),
            P(("row", "seq"), None),
            P(("row", "seq")),
            P(("row", "seq")),
            P(("row", "seq")),
            P(("row", "seq")),
            P(("row", "seq")),
            P(("row", "seq")),
            P(),
        ),
        check_vma=False,
    )
```

```python
import math

import jax
import jax.numpy as jnp
from jax import lax
from jax.experimental import pallas as pl
from jax.experimental.pallas import tpu as pltpu
from jax.sharding import PartitionSpec as P

finest = lax.Precision.HIGHEST


def swap_out(part):
    count = lax.axis_size("seq")
    shape = part.shape
    cut = part.reshape(shape[:2] + (count, shape[2] // count) + shape[3:])
    return lax.all_to_all(jnp.moveaxis(cut, 2, 0), "seq", 0, 0)


def swap_back(part):
    whole = jnp.moveaxis(lax.all_to_all(part, "seq", 0, 0), 0, 2)
    shape = whole.shape
    return whole.reshape(shape[:2] + (shape[2] * shape[3],) + shape[4:])


def chain(first, factors, pieces, reverse):
    def step(total, block):
        factor, piece = block
        spread = factor.reshape(factor.shape + (1,) * (piece.ndim - factor.ndim))
        return spread * total + piece, total

    return lax.scan(step, first, (factors, pieces), reverse=reverse)


def normed(values, gain, shift):
    centre = jnp.mean(values, axis=-1, keepdims=True)
    centred = values - centre
    spread = jnp.mean(centred * centred, axis=-1, keepdims=True)
    return centred * lax.rsqrt(spread + 1e-05) * gain + shift


def features(vectors, rand_feat):
    unit = vectors * lax.rsqrt(jnp.sum(vectors * vectors, axis=-1, keepdims=True) + 1e-06)
    mapped = jnp.einsum("sthe,hfe->sthf", unit, rand_feat, precision=finest)
    return jnp.exp(mapped - 0.5) / math.sqrt(rand_feat.shape[1])


def intra(projected, gate_bias, rand_feat):
    heads, feat, head_dim = rand_feat.shape
    seq_count, block_len, _ = projected.shape
    model_width = heads * head_dim
    query = projected[..., :model_width].reshape(seq_count, block_len, heads, head_dim)
    key_vec = projected[..., model_width : 2 * model_width].reshape(
        seq_count, block_len, heads, head_dim
    )
    value = projected[..., 2 * model_width : 3 * model_width].reshape(
        seq_count, block_len, heads, head_dim
    )
    logit = projected[..., 3 * model_width :] + gate_bias
    log_keep = -jax.nn.softplus(-logit)
    write = jax.nn.sigmoid(-logit)
    cumul = jnp.cumsum(log_keep, axis=1)
    q_feat = features(query, rand_feat)
    k_feat = features(key_vec, rand_feat)
    by_head = jnp.transpose(cumul, (0, 2, 1))
    differ = by_head[:, :, :, None] - by_head[:, :, None, :]
    lower = jnp.arange(block_len)[:, None] >= jnp.arange(block_len)[None, :]
    decay = jnp.where(lower, jnp.exp(jnp.where(lower, differ, 0.0)), 0.0)
    decay = decay * jnp.transpose(write, (0, 2, 1))[:, :, None, :]
    scores = jnp.einsum("sthf,suhf->shtu", q_feat, k_feat, precision=finest) * decay
    numer = jnp.einsum("shtu,suhe->sthe", scores, value, precision=finest)
    denom = jnp.transpose(jnp.sum(scores, axis=-1), (0, 2, 1))
    ending = cumul[:, -1, :]
    weighted = k_feat * (jnp.exp(ending[:, None, :] - cumul) * write)[..., None]
    local_state = jnp.einsum("suhf,suhe->shfe", weighted, value, precision=finest)
    local_norm = jnp.sum(weighted, axis=1)
    return (numer, denom, cumul, q_feat, ending, local_state, local_norm)


def inter(numer, denom, cumul, q_feat, state, norm):
    growth = jnp.exp(cumul)
    full_num = numer + growth[..., None] * jnp.einsum(
        "sthf,shfe->sthe", q_feat, state, precision=finest
    )
    full_den = denom + growth * jnp.einsum("sthf,shf->sth", q_feat, norm, precision=finest)
    merged = full_num / full_den[..., None]
    return merged.reshape(merged.shape[0], merged.shape[1], -1)


def mixer(projected, gate_bias, rand_feat, state, norm):
    numer, denom, cumul, q_feat, ending, local_state, local_norm = intra(
        projected, gate_bias, rand_feat
    )
    output = inter(numer, denom, cumul, q_feat, state, norm)
    carry = jnp.exp(ending)
    return (
        output,
        carry[:, :, None, None] * state + local_state,
        carry[:, :, None] * norm + local_norm,
    )


def matmul(left, right):
    return jnp.dot(left, right, preferred_element_type=jnp.float32)


def left_inner(left, right):
    return lax.dot_general(
        left, right, (((0,), (0,)), ((), ())), preferred_element_type=jnp.float32
    )


def right_inner(left, right):
    return lax.dot_general(
        left, right, (((1,), (1,)), ((), ())), preferred_element_type=jnp.float32
    )


def body(
    tokens,
    w_query,
    w_key,
    w_value,
    w_gate,
    w_out,
    w_up,
    w_down,
    gain_one,
    shift_one,
    gain_two,
    shift_two,
    bias_up,
    bias_down,
    gate_bias,
    start_state,
    start_norm,
    rand_feat,
    out_grad,
    state_grad,
    norm_grad,
):
    bf = jnp.bfloat16
    gathered = (
        lax.all_gather(w_query.astype(bf), ("row", "seq"), axis=0, tiled=True),
        lax.all_gather(w_key.astype(bf), ("row", "seq"), axis=0, tiled=True),
        lax.all_gather(w_value.astype(bf), ("row", "seq"), axis=0, tiled=True),
        lax.all_gather(w_gate.astype(bf), ("row", "seq"), axis=0, tiled=True),
        lax.all_gather(w_out.astype(bf), ("row", "seq"), axis=0, tiled=True),
        lax.all_gather(w_up.astype(bf), ("row", "seq"), axis=0, tiled=True),
        lax.all_gather(w_down.astype(bf), ("row", "seq"), axis=0, tiled=True),
        lax.all_gather(gain_one.astype(bf), ("row", "seq"), axis=0, tiled=True),
        lax.all_gather(shift_one.astype(bf), ("row", "seq"), axis=0, tiled=True),
        lax.all_gather(gain_two.astype(bf), ("row", "seq"), axis=0, tiled=True),
        lax.all_gather(shift_two.astype(bf), ("row", "seq"), axis=0, tiled=True),
        lax.all_gather(bias_up.astype(bf), ("row", "seq"), axis=0, tiled=True),
        lax.all_gather(bias_down.astype(bf), ("row", "seq"), axis=0, tiled=True),
    )
    (
        query_half,
        key_half,
        value_half,
        gate_half,
        out_half,
        up_half,
        down_half,
        gain_first,
        shift_first,
        gain_second,
        shift_second,
        up_bias,
        down_bias,
    ) = gathered
    gain_first = gain_first.astype(jnp.float32)
    shift_first = shift_first.astype(jnp.float32)
    gain_second = gain_second.astype(jnp.float32)
    shift_second = shift_second.astype(jnp.float32)
    local_seqs, block_len, model_width = tokens.shape
    row_total = local_seqs * block_len
    token_rows = tokens.reshape(row_total, model_width).astype(jnp.float32)
    first_half = normed(token_rows, gain_first, shift_first).astype(bf)
    input_weight = jnp.concatenate([query_half, key_half, value_half, gate_half], axis=1)
    proj_blocks = matmul(first_half, input_weight).reshape(local_seqs, block_len, -1)
    numer, denom, cumul, q_feat, ending, local_state, local_norm = intra(
        proj_blocks, gate_bias, rand_feat
    )
    factors = jnp.exp(lax.all_gather(ending, "seq"))
    slice_len = state_grad.shape[2]
    offset = lax.axis_index("seq") * slice_len
    state_slice = lax.dynamic_slice_in_dim(start_state, offset, slice_len, 2)
    norm_slice = lax.dynamic_slice_in_dim(start_norm, offset, slice_len, 2)
    final_state, states = chain(state_slice, factors, swap_out(local_state), False)
    final_norm, norms = chain(norm_slice, factors, swap_out(local_norm), False)
    state_in = swap_back(states)
    norm_in = swap_back(norms)
    attended = inter(numer, denom, cumul, q_feat, state_in, norm_in)
    attended_half = attended.reshape(row_total, model_width).astype(bf)
    mixed = token_rows + matmul(attended_half, out_half)
    second_half = normed(mixed, gain_second, shift_second).astype(bf)
    pre_act = matmul(second_half, up_half) + up_bias.astype(jnp.float32)
    hidden_half = jax.nn.gelu(pre_act).astype(bf)
    result = mixed + matmul(hidden_half, down_half) + down_bias.astype(jnp.float32)
    grad_rows = out_grad.reshape(row_total, model_width)
    grad_float = grad_rows.astype(jnp.float32)
    grad_bias_down = jnp.sum(grad_float, axis=0)
    grad_down = left_inner(hidden_half, grad_rows)
    grad_hidden = right_inner(grad_rows, down_half)
    _, gelu_back = jax.vjp(jax.nn.gelu, pre_act)
    grad_pre_half = gelu_back(grad_hidden)[0].astype(bf)
    grad_bias_up = jnp.sum(grad_pre_half.astype(jnp.float32), axis=0)
    grad_up = left_inner(second_half, grad_pre_half)
    grad_second = right_inner(grad_pre_half, up_half)
    _, second_back = jax.vjp(normed, mixed, gain_second, shift_second)
    mixed_from_norm, grad_gain_two, grad_shift_two = second_back(grad_second)
    grad_mixed = grad_float + mixed_from_norm
    grad_mixed_half = grad_mixed.astype(bf)
    grad_out = left_inner(attended_half, grad_mixed_half)
    grad_att = right_inner(grad_mixed_half, out_half).reshape(local_seqs, block_len, model_width)
    _, inter_back = jax.vjp(
        lambda state, norm: inter(numer, denom, cumul, q_feat, state, norm), state_in, norm_in
    )
    own_state_grad, own_norm_grad = inter_back(grad_att)
    start_state_grad, state_carries = chain(state_grad, factors, swap_out(own_state_grad), True)
    start_norm_grad, norm_carries = chain(norm_grad, factors, swap_out(own_norm_grad), True)
    carry_state = swap_back(state_carries)
    carry_norm = swap_back(norm_carries)

    def mixer_local(proj_part, bias_part):
        return mixer(proj_part, bias_part, rand_feat, state_in, norm_in)

    _, mixer_back = jax.vjp(mixer_local, proj_blocks, gate_bias)
    grad_proj, grad_bias_gate = mixer_back((grad_att, carry_state, carry_norm))
    grad_proj_half = grad_proj.reshape(row_total, -1).astype(bf)
    grad_joined = left_inner(first_half, grad_proj_half)
    grad_first = right_inner(grad_proj_half, input_weight)
    _, first_back = jax.vjp(normed, token_rows, gain_first, shift_first)
    tokens_from_norm, grad_gain_one, grad_shift_one = first_back(grad_first)
    input_grad = (grad_mixed + tokens_from_norm).astype(bf).reshape(tokens.shape)
    grad_query = grad_joined[:, :model_width]
    grad_key = grad_joined[:, model_width : 2 * model_width]
    grad_value = grad_joined[:, 2 * model_width : 3 * model_width]
    grad_gate = grad_joined[:, 3 * model_width :]
    owned = (
        lax.psum_scatter(grad_query, ("row", "seq"), scatter_dimension=0, tiled=True),
        lax.psum_scatter(grad_key, ("row", "seq"), scatter_dimension=0, tiled=True),
        lax.psum_scatter(grad_value, ("row", "seq"), scatter_dimension=0, tiled=True),
        lax.psum_scatter(grad_gate, ("row", "seq"), scatter_dimension=0, tiled=True),
        lax.psum_scatter(grad_out, ("row", "seq"), scatter_dimension=0, tiled=True),
        lax.psum_scatter(grad_up, ("row", "seq"), scatter_dimension=0, tiled=True),
        lax.psum_scatter(grad_down, ("row", "seq"), scatter_dimension=0, tiled=True),
        lax.psum_scatter(grad_gain_one, ("row", "seq"), scatter_dimension=0, tiled=True),
        lax.psum_scatter(grad_shift_one, ("row", "seq"), scatter_dimension=0, tiled=True),
        lax.psum_scatter(grad_gain_two, ("row", "seq"), scatter_dimension=0, tiled=True),
        lax.psum_scatter(grad_shift_two, ("row", "seq"), scatter_dimension=0, tiled=True),
        lax.psum_scatter(grad_bias_up, ("row", "seq"), scatter_dimension=0, tiled=True),
        lax.psum_scatter(grad_bias_down, ("row", "seq"), scatter_dimension=0, tiled=True),
    )
    gate_total = lax.psum(grad_bias_gate, ("row", "seq"))
    return (
        result.astype(bf).reshape(tokens.shape),
        final_state,
        final_norm,
        input_grad,
        start_state_grad,
        start_norm_grad,
        owned[0],
        owned[1],
        owned[2],
        owned[3],
        owned[4],
        owned[5],
        owned[6],
        owned[7],
        owned[8],
        owned[9],
        owned[10],
        owned[11],
        owned[12],
        gate_total,
    )


bf = jnp.bfloat16
f32 = jnp.float32
MESH = pl.DeviceIdType.MESH
LANES = 128
ROWS = 16
SUMMED = 16
VMEM = 60 * 2**20


def here():
    row, seq = lax.axis_index("row"), lax.axis_index("seq")
    return row // 2, row % 2, seq // 2, seq % 2


def place(y, x, z, core):
    return (y * 2 + x, z * 2 + core)


def greet(devices):
    barrier = pltpu.get_barrier_semaphore()
    for device in devices:
        pl.semaphore_signal(barrier, inc=1, device_id=device, device_id_type=MESH)
    return lambda: pl.semaphore_wait(barrier, len(devices))


class Post:
    def __init__(self, send, recv):
        self.send, self.recv, self.count, self.sent = send, recv, 0, []

    def __call__(self, src, dst, device):
        slot = self.count
        self.count += 1
        copy = pltpu.make_async_remote_copy(
            src_ref=src,
            dst_ref=dst,
            send_sem=self.send.at[slot],
            recv_sem=self.recv.at[slot],
            device_id=device,
            device_id_type=MESH,
        )
        copy.start()
        self.sent.append(copy)
        return copy

    def close(self):
        for copy in self.sent:
            copy.wait_send()


def dot(left, right):
    return jnp.dot(left, right, preferred_element_type=f32)


def dot_nt(left, right):
    return lax.dot_general(left, right, (((1,), (1,)), ((), ())), preferred_element_type=f32)


def dot_tn(left, right):
    return lax.dot_general(left, right, (((0,), (0,)), ((), ())), preferred_element_type=f32)


def halves(value):
    high = value.astype(bf)
    return high, (value - high.astype(f32)).astype(bf)


def thirds(value):
    high = value.astype(bf)
    rest = value - high.astype(f32)
    middle = rest.astype(bf)
    return high, middle, (rest - middle.astype(f32)).astype(bf)


def fine(product, left, right):
    left_high, left_low = halves(left)
    right_high, right_low = halves(right)
    return product(left_high, right_high) + product(left_low, right_high) + product(left_high, right_low)


def gather_kernel(
    wq, wk, wv, wo, w1, w2, gate, small, tokens, grads, state_grad,
    ga, gb, x_own, dy_own, sg,
    send, recv,
):
    y, x, z, core = here()
    depth = tokens.shape[0]
    row, row_x, row_y, row_d = y * 2 + x, y * 2 + 1 - x, (1 - y) * 2 + x, (1 - y) * 2 + 1 - x
    sibling = place(y, x, z, 1 - core)
    beside_x, beside_y = place(y, 1 - x, z, core), place(1 - y, x, z, core)
    column = [place(y, x, (z + k) % depth, core) for k in range(1, depth)]
    other = [place(y, x, (z + k) % depth, 1 - core) for k in range(depth)]
    ready = greet([beside_x, beside_y] + column + other)
    width = wq.shape[1] // 2
    half = 3 * width + LANES
    for part in range(2):
        for index, weight in enumerate((wq, wk, wv)):
            ga[row, z, core, :, part * half + index * width : part * half + (index + 1) * width] = (
                weight[:, part * width : (part + 1) * width].astype(bf)
            )
        ga[row, z, core, :, part * half + 3 * width : (part + 1) * half] = gate[
            :, part * LANES : (part + 1) * LANES
        ].astype(bf)
    ga[row, z, core, :, 2 * half :] = small[...]
    model = wo.shape[1]
    groups = w1.shape[1] // model
    gb[row, z, core, 0:ROWS, :] = wo[...].astype(bf)
    for group in range(groups):
        gb[row, z, core, ROWS * (group + 1) : ROWS * (group + 2), :] = w1[
            :, group * model : (group + 1) * model
        ].astype(bf)
    gb[row, z, core, ROWS * (groups + 1) :, :] = w2[...].astype(bf)
    x_own[z] = tokens[z]
    dy_own[z] = grads[z]
    heads = state_grad.shape[1] // 2
    sg[2 * z + core] = state_grad[z, pl.ds(heads * core, heads)]
    ready()
    post = Post(send, recv)

    def along(buffer):
        mine = buffer.at[row, z, core]
        return [post(mine, mine, device) for device in column]

    def across(buffer, k):
        mine = buffer.at[row, (z - k) % depth, core]
        return post(mine, mine, beside_x), post(mine, mine, beside_y)

    def swap(source, target):
        return [
            post(source.at[(z + k) % depth], target.at[z], column[k - 1]) for k in range(1, depth)
        ]

    def spread(buffer, down):
        over = [across(buffer, 0)]
        for k in range(1, depth):
            down[k - 1].wait_recv()
            over.append(across(buffer, k))
        relay = []
        for k in range(depth):
            level = (z - k) % depth
            if k < depth // 2:
                over[k][0].wait_recv()
                piece = buffer.at[row_x, level, core]
                relay.append(post(piece, piece, beside_y))
            else:
                over[k][1].wait_recv()
                piece = buffer.at[row_y, level, core]
                relay.append(post(piece, piece, beside_x))
        for k in range(depth):
            over[k][1 if k < depth // 2 else 0].wait_recv()
        return relay

    def pass_on(buffer, cuts):
        taken = []
        for row_from in (row, row_x, row_y, row_d):
            for cut in cuts:
                piece = buffer.at[(row_from, slice(None), core, slice(None)) + cut]
                taken.append(post(piece, piece, sibling))
        return taken

    down_a = along(ga)
    came_x = swap(tokens, x_own)
    down_b = along(gb)
    relay_a = spread(ga, down_a)
    came_y = swap(grads, dy_own)
    came_s = []
    for k in range(depth):
        for flip in range(2):
            if k or flip:
                level, to = (z + k) % depth, core if flip == 0 else 1 - core
                came_s.append(
                    post(
                        state_grad.at[level, pl.ds(heads * to, heads)],
                        sg.at[2 * z + core],
                        place(y, x, level, to),
                    )
                )
    for copy in relay_a:
        copy.wait_recv()
    cut_half = (pl.ds(pl.multiple_of((1 - core) * half, LANES), half),)
    cut_small = (pl.ds(2 * half, model),)
    sib_a = pass_on(ga, (cut_half, cut_small))
    relay_b = spread(gb, down_b)
    for copy in relay_b:
        copy.wait_recv()
    sib_b = pass_on(gb, ((slice(None),),))
    for copy in sib_a + sib_b + came_x + came_y + came_s:
        copy.wait_recv()
    post.close()


def norm_stats(values):
    centred = values - jnp.mean(values, axis=-1, keepdims=True)
    scale = lax.rsqrt(jnp.mean(centred * centred, axis=-1, keepdims=True) + 1e-05)
    return centred * scale, scale


def norm_back(cotangent, unit, scale, gain):
    inner = cotangent * gain
    return scale * (
        inner
        - jnp.mean(inner, axis=-1, keepdims=True)
        - unit * jnp.mean(inner * unit, axis=-1, keepdims=True)
    )


def small_rows(ga, start):
    part = ga[:, :, :, :, start:].astype(f32)
    return jnp.sum(part.reshape(-1, *part.shape[3:]), axis=0)


def iota_pair(size):
    return (
        lax.broadcasted_iota(jnp.int32, (size, size), 0),
        lax.broadcasted_iota(jnp.int32, (size, size), 1),
    )


def head_ones(size, head_dim):
    first, second = iota_pair(size)
    return jnp.where(first // head_dim == second // head_dim, 1.0, 0.0).astype(bf)


def lower_ones(size):
    first, second = iota_pair(size)
    return jnp.where(first >= second, 1.0, 0.0).astype(bf)


def group_sum(values, ones):
    high, low = halves(values)
    return dot(high, ones) + dot(low, ones)


def unit_features(vectors, ones, feat_high, feat_low, feat):
    inverse = lax.rsqrt(group_sum(vectors * vectors, ones) + 1e-06)
    unit = vectors * inverse
    high, low = halves(unit)
    mapped = dot_nt(high, feat_high) + dot_nt(low, feat_high) + dot_nt(high, feat_low)
    return unit, inverse, jnp.exp(mapped - (0.5 + 0.5 * math.log(feat)))


def gates(logit, lower):
    tail = jnp.exp(-jnp.abs(logit))
    log_keep = jnp.minimum(logit, 0.0) - jnp.log1p(tail)
    write = jnp.where(logit >= 0, tail, 1.0) / (1.0 + tail)
    keep = jnp.where(logit >= 0, 1.0, tail) / (1.0 + tail)
    cumul = sum(dot(lower, part) for part in thirds(log_keep))
    return write, keep, cumul


def head_lanes(values, head, head_dim):
    pair = values[:, (head // 2) * LANES : (head // 2 + 1) * LANES]
    return pltpu.roll(pair, head_dim, 1) if head % 2 else pair


def join_heads(parts, head_dim):
    lane = lax.broadcasted_iota(jnp.int32, parts[0].shape, 1)
    return jnp.concatenate(
        [
            jnp.where(lane < head_dim, parts[2 * i], pltpu.roll(parts[2 * i + 1], head_dim, 1))
            for i in range(len(parts) // 2)
        ],
        axis=1,
    )


def decays(cumul_turned, write_turned, cumul, head, seen):
    gap = cumul[:, head : head + 1] - cumul_turned[head : head + 1, :]
    return jnp.exp(jnp.where(seen, gap, -1e30)) * write_turned[head : head + 1, :]


def mix_kernel(
    ga, x_own, spread, gate_bias, start,
    proj, first, attended, states, raw,
    ones_ref, lower_ref, feat_high, feat_low, mine, send, recv,
):
    y, x, z, core = here()
    sibling = place(y, x, z, 1 - core)
    ready = greet([sibling])
    depth, block, model = x_own.shape
    heads, feat, _ = start.shape
    width = mine.shape[3]
    head_dim = width // heads
    half = 3 * width + LANES
    chunk = 2 * block
    vectors = small_rows(ga, 2 * half)
    values = x_own[...].astype(f32).reshape(depth * block, model)
    unit, _ = norm_stats(values)
    first[core] = (unit * vectors[0:1] + vectors[1:2]).astype(bf).reshape(depth, block, model)
    ones_ref[...] = head_ones(width, head_dim)
    lower_ref[...] = lower_ones(chunk)
    feat_high[...], feat_low[...] = halves(spread[...])
    states[0] = start[...]
    ready()
    post = Post(send, recv)
    post(first.at[core], first.at[core], sibling).wait_recv()
    columns = pl.ds(pl.multiple_of(core * half, LANES), half)

    def step(i, carry):
        weight = ga[:, :, :, :, columns].reshape(model, half)
        rows = first[:, i].reshape(chunk, model)
        result = dot(rows, weight)
        logit = result[:, 3 * width :] + gate_bias[...]
        proj[:, i, :, : 3 * width] = result[:, : 3 * width].reshape(2, block, 3 * width)
        proj[:, i, :, 3 * width :] = logit.reshape(2, block, LANES)
        ones, lower = ones_ref[...], lower_ref[...]
        _, _, q_feat = unit_features(result[:, :width], ones, feat_high[...], feat_low[...], feat)
        _, _, k_feat = unit_features(
            result[:, width : 2 * width], ones, feat_high[...], feat_low[...], feat
        )
        write, _, cumul = gates(logit, lower)
        ending = cumul[chunk - 1 : chunk, :]
        growth = jnp.exp(cumul)
        fading = jnp.exp(ending - cumul) * write
        shrink = jnp.exp(ending)
        cumul_turned, write_turned = cumul.T, write.T
        row_at, column_at = iota_pair(chunk)
        seen = row_at >= column_at
        lane = lax.broadcasted_iota(jnp.int32, (chunk, LANES), 1)
        outs = []
        for head in range(heads):
            cut = slice(head * feat, (head + 1) * feat)
            q_head, k_head = q_feat[:, cut], k_feat[:, cut]
            value = head_lanes(result[:, 2 * width : 3 * width], head, head_dim)
            value = jnp.where(lane < head_dim, value, jnp.where(lane == head_dim, 1.0, 0.0))
            decay = decays(cumul_turned, write_turned, cumul, head, seen)
            scores = fine(dot_nt, q_head, k_head) * decay
            state = states[i, head]
            total = fine(dot, scores, value) + growth[:, head : head + 1] * fine(dot, q_head, state)
            raw[head, :, i] = total.reshape(2, block, LANES)
            outs.append(total * (1.0 / total[:, head_dim : head_dim + 1]))
            weighted = k_head * fading[:, head : head + 1]
            states[i + 1, head] = shrink[:, head : head + 1] * state + fine(dot_tn, weighted, value)
        mine[:, i] = join_heads(outs, head_dim).astype(bf).reshape(2, block, width)
        return carry

    lax.fori_loop(0, depth, step, 0)
    lanes = pl.ds(pl.multiple_of(core * width, LANES), width)
    sent = post(mine.at[1 - core], attended.at[:, :, lanes], sibling)
    attended[:, :, lanes] = mine[core]
    sent.wait_recv()
    post.close()


def ff_kernel(
    ga, gb, x_own, dy_own, attended,
    result, parts, grad_mixed, grad_att, sums,
    second, hidden_sum, grad_second, grad_full, send, recv,
):
    y, x, z, core = here()
    sibling = place(y, x, z, 1 - core)
    ready = greet([sibling])
    depth, block, model = x_own.shape
    rows = depth * block
    width = grad_att.shape[3]
    groups = (gb.shape[3] - ROWS) // (2 * ROWS)
    down_at = ROWS * (groups + 1)
    per = gb.shape[3] - down_at
    vectors = small_rows(ga, ga.shape[4] - model)
    weight_out = gb[:, :, :, 0:ROWS, :].reshape(model, model)
    att = attended[...].reshape(rows, model)
    mixed = x_own[...].astype(f32).reshape(rows, model) + dot(att, weight_out)
    unit, scale = norm_stats(mixed)
    second[...] = (unit * vectors[2:3] + vectors[3:4]).astype(bf)
    hidden_sum[...] = mixed + vectors[4:5]
    grad_second[...] = jnp.zeros_like(grad_second)
    sums[...] = jnp.zeros_like(sums)
    level = gb.shape[0] // groups
    for group in range(groups):
        up_rows = slice(ROWS * (group + 1), ROWS * (group + 2))
        weight_up = gb[:, :, :, up_rows, :].reshape(model, model)
        owners = slice(group * level, (group + 1) * level)
        weight_down = gb[owners, :, :, down_at:, :].reshape(model, model)
        given = dy_own[...].reshape(rows, model)
        h2 = second[...]
        before = dot(h2, weight_up) + vectors[5 + group : 6 + group]
        square = before * before
        inner = jnp.tanh(before * (0.7978845608028654 + 0.035677408136300125 * square))
        half_up = 0.5 + 0.5 * inner
        hidden = (before * half_up).astype(bf)
        slope = half_up + before * (0.5 - 0.5 * inner * inner) * (
            0.7978845608028654 + 0.10703222440890037 * square
        )
        hidden_sum[...] += dot(hidden, weight_down)
        grad_before = dot_nt(given, weight_down) * slope
        sums[5 + group : 6 + group, :] = jnp.sum(grad_before, axis=0, keepdims=True)
        grad_before = grad_before.astype(bf)
        parts[owners, :, :, down_at:, :] = (
            dot_tn(hidden, given).astype(bf).reshape(level, depth, 2, per, model)
        )
        parts[:, :, :, up_rows, :] = (
            dot_tn(h2, grad_before).astype(bf).reshape(-1, depth, 2, ROWS, model)
        )
        grad_second[...] += dot_nt(grad_before, weight_up)
    result[...] = hidden_sum[...].astype(bf).reshape(depth, block, model)
    given = dy_own[...].reshape(rows, model).astype(f32)
    cotangent = grad_second[...]
    total = given + norm_back(cotangent, unit, scale, vectors[2:3])
    grad_mixed[...] = total.reshape(depth, block, model)
    sums[2:3, :] = jnp.sum(cotangent * unit, axis=0, keepdims=True)
    sums[3:4, :] = jnp.sum(cotangent, axis=0, keepdims=True)
    sums[4:5, :] = jnp.sum(given, axis=0, keepdims=True)
    total = total.astype(bf)
    parts[:, :, :, 0:ROWS, :] = dot_tn(att, total).astype(bf).reshape(-1, depth, 2, ROWS, model)
    grad_full[...] = dot_nt(total, weight_out).reshape(depth, block, model)
    ready()
    post = Post(send, recv)
    theirs = grad_full.at[:, :, pl.ds(pl.multiple_of((1 - core) * width, LANES), width)]
    sent = post(theirs, grad_att.at[core], sibling)
    grad_att[core] = grad_full[:, :, pl.ds(pl.multiple_of(core * width, LANES), width)]
    sent.wait_recv()
    post.close()


def unmix_kernel(
    ga, x_own, spread, proj, first, states, raw, grad_att, sg, grad_mixed, sums_in,
    input_grad, start_grad, parts, sums,
    ones_ref, lower_ref, feat_high, feat_low, grad_proj, grad_feat, grad_first, landed, send, recv,
):
    y, x, z, core = here()
    sibling = place(y, x, z, 1 - core)
    ready = greet([sibling])
    depth, block, model = x_own.shape
    heads, feat, _ = start_grad.shape
    width = grad_att.shape[3]
    head_dim = width // heads
    half = 3 * width + LANES
    chunk = 2 * block
    columns = pl.ds(pl.multiple_of(core * half, LANES), half)
    ones_ref[...] = head_ones(width, head_dim)
    lower_ref[...] = lower_ones(chunk)
    feat_high[...], feat_low[...] = halves(spread[...])
    slices = sg.shape[0]
    for piece in range(slices):
        span = feat // slices
        start_grad[:, piece * span : (piece + 1) * span, :] = sg[piece].astype(f32)

    def step(back, bias_sum):
        i = depth - 1 - back
        whole = proj[:, i].reshape(chunk, half)
        ones, lower = ones_ref[...], lower_ref[...]
        query, key_vec = whole[:, :width], whole[:, width : 2 * width]
        q_unit, q_inverse, q_feat = unit_features(
            query, ones, feat_high[...], feat_low[...], feat
        )
        k_unit, k_inverse, k_feat = unit_features(
            key_vec, ones, feat_high[...], feat_low[...], feat
        )
        write, keep, cumul = gates(whole[:, 3 * width :], lower)
        ending = cumul[chunk - 1 : chunk, :]
        growth = jnp.exp(cumul)
        fading = jnp.exp(ending - cumul) * write
        shrink = jnp.exp(ending)
        cumul_turned, write_turned = cumul.T, write.T
        row_at, column_at = iota_pair(chunk)
        seen = row_at >= column_at
        lane = lax.broadcasted_iota(jnp.int32, (chunk, LANES), 1)
        given = grad_att[:, i].reshape(chunk, width)
        value_grads = []
        shares = jnp.zeros((chunk, LANES), f32)
        endings = jnp.zeros((1, LANES), f32)
        for head in range(heads):
            cut = slice(head * feat, (head + 1) * feat)
            q_head, k_head = q_feat[:, cut], k_feat[:, cut]
            value = head_lanes(whole[:, 2 * width : 3 * width], head, head_dim)
            value = jnp.where(lane < head_dim, value, jnp.where(lane == head_dim, 1.0, 0.0))
            total = raw[head, :, i].reshape(chunk, LANES)
            inverse = 1.0 / total[:, head_dim : head_dim + 1]
            cotangent = jnp.where(lane < head_dim, head_lanes(given, head, head_dim), 0.0) * inverse
            against = -jnp.sum(cotangent * total, axis=1, keepdims=True) * inverse
            cotangent = jnp.where(lane == head_dim, against, cotangent)
            cot_grown = cotangent * growth[:, head : head + 1]
            state = states[i, head]
            carry = start_grad[head]
            decay = decays(cumul_turned, write_turned, cumul, head, seen)
            scores = fine(dot_nt, q_head, k_head) * decay
            grad_scores = fine(dot_nt, cotangent, value) * decay
            fade = fading[:, head : head + 1]
            value_grads.append(fine(dot_tn, scores, cotangent) + fade * fine(dot, k_head, carry))
            grad_q = fine(dot, grad_scores, k_head) + fine(dot_nt, cot_grown, state)
            grad_k = fine(dot_tn, grad_scores, q_head) + fade * fine(dot_nt, value, carry)
            grad_q = grad_q * q_head
            grad_k = grad_k * k_head
            share = jnp.sum(grad_k, axis=1, keepdims=True)
            shares = jnp.where(lane == head, share, shares)
            after = jnp.sum(
                jnp.sum(states[i + 1, head] * carry, axis=0, keepdims=True), axis=1, keepdims=True
            )
            endings = jnp.where(lane[0:1] == head, after, endings)
            grad_feat[0, :, cut] = grad_q
            grad_feat[1, :, cut] = grad_k
            start_grad[head] = shrink[:, head : head + 1] * carry + fine(dot_tn, q_head, cot_grown)
        later = sum(dot_tn(lower, part) for part in thirds(shares))
        grad_logit = (endings - later) * write - shares * keep
        pieces = []
        for index, (unit, inverse) in enumerate(((q_unit, q_inverse), (k_unit, k_inverse))):
            high, low = halves(grad_feat[index])
            grad_unit = (
                dot(high, feat_high[...]) + dot(low, feat_high[...]) + dot(high, feat_low[...])
            )
            along = group_sum(unit * grad_unit, ones)
            pieces.append((inverse * (grad_unit - unit * along)).astype(bf))
        pieces.append(join_heads(value_grads, head_dim).astype(bf))
        pieces.append(grad_logit.astype(bf))
        grad_proj[:, i] = jnp.concatenate(pieces, axis=1).reshape(2, block, half)
        return bias_sum + jnp.sum(grad_logit, axis=0, keepdims=True)

    bias_sum = lax.fori_loop(0, depth, step, jnp.zeros((1, LANES), f32))
    weight = ga[:, :, :, :, columns].reshape(model, half)
    theirs = grad_proj[1 - core].reshape(depth * block, half)
    grad_first[...] = dot_nt(theirs, weight).reshape(depth, block, model)
    ready()
    post = Post(send, recv)
    sent = post(grad_first, landed, sibling)
    joined = dot_tn(
        first[...].reshape(2 * depth * block, model), grad_proj[...].reshape(2 * depth * block, half)
    )
    parts[...] = joined.astype(bf).reshape(parts.shape)
    ours = grad_proj[core].reshape(depth * block, half)
    partial = dot_nt(ours, weight)
    values = x_own[...].astype(f32).reshape(depth * block, model)
    unit, scale = norm_stats(values)
    vectors = small_rows(ga, 2 * half)
    sent.wait_recv()
    cotangent = partial + landed[...].reshape(depth * block, model)
    total = grad_mixed[...].reshape(depth * block, model) + norm_back(
        cotangent, unit, scale, vectors[0:1]
    )
    input_grad[...] = total.astype(bf).reshape(depth, block, model)
    sums[...] = sums_in[...]
    sums[0:1, :] = jnp.sum(cotangent * unit, axis=0, keepdims=True)
    sums[1:2, :] = jnp.sum(cotangent, axis=0, keepdims=True)
    for part in range(2):
        share = jnp.where(core == part, 1.0, 0.0)
        sums[9 + part : 10 + part, 0:LANES] = bias_sum * share
    post.close()


def scatter_kernel(
    parts_a, parts_b, sums_in, result_own, input_own, final, start_grad,
    grad_q, grad_k, grad_v, grad_gate, grad_out, grad_up, grad_down, sums, result, input_grad, final_out, start_out,
    acc_a, acc_b, from_sib, in_a1, in_b1, in_a2, in_b2, in_a3, in_b3, last_a, final_half, start_half, total, in_s, send, recv,
):
    y, x, z, core = here()
    depth = result_own.shape[0]
    row = y * 2 + x
    sibling = place(y, x, z, 1 - core)
    beside_x, beside_y = place(y, 1 - x, z, core), place(1 - y, x, z, core)
    column = [place(y, x, (z + k) % depth, core) for k in range(1, depth)]
    other = [place(y, x, (z + k) % depth, 1 - core) for k in range(depth)]
    ready = greet([beside_x, beside_y] + column + other)
    heads, feat, _ = final.shape
    final_half[...] = final[...].astype(bf)
    start_half[...] = start_grad[...].astype(bf)
    slices = 2 * depth
    span = feat // slices
    own_slice = pl.ds(pl.multiple_of((2 * z + core) * span, ROWS), span)
    own_heads = pl.ds(heads * core, heads)
    final_out[z, own_heads] = final_half[:, own_slice, :]
    start_out[z, own_heads] = start_half[:, own_slice, :]
    result[z] = result_own[z]
    input_grad[z] = input_own[z]
    total[0] = sums_in[0]
    ready()
    post = Post(send, recv)
    sib_b = post(parts_b.at[:, :, 1 - core], from_sib, sibling)
    sib_s = post(total.at[0], in_s.at[0], sibling)
    nearer = range(depth // 2)
    further = range(depth // 2, depth)

    def level(k):
        return (z + k) % depth

    def first_hop(acc, landing):
        out = []
        for k in nearer:
            for side in range(2):
                out.append(
                    post(acc.at[side * 2 + 1 - x, level(k)], landing.at[0, k, side], beside_x)
                )
        for k in further:
            for side in range(2):
                out.append(
                    post(
                        acc.at[(1 - y) * 2 + side, level(k)],
                        landing.at[1, k - depth // 2, side],
                        beside_y,
                    )
                )
        return out

    def add(acc, at_row, at_level, more):
        acc[at_row, at_level] = (acc[at_row, at_level].astype(f32) + more.astype(f32)).astype(bf)

    def second_hop(acc, landed, landing, copies):
        for copy in copies:
            copy.wait_recv()
        out = []
        for k in nearer:
            for side in range(2):
                add(acc, side * 2 + x, level(k), landed[0, k, side])
            out.append(post(acc.at[(1 - y) * 2 + x, level(k)], landing.at[0, k], beside_y))
        for k in further:
            for side in range(2):
                add(acc, y * 2 + side, level(k), landed[1, k - depth // 2, side])
            out.append(
                post(acc.at[y * 2 + 1 - x, level(k)], landing.at[1, k - depth // 2], beside_x)
            )
        return out

    def third_hop(acc, landed, landing, copies):
        for copy in copies:
            copy.wait_recv()
        for k in range(depth):
            add(acc, row, level(k), landed[0 if k in nearer else 1, k % (depth // 2)])
        return [
            post(acc.at[row, level(k)], landing.at[k - 1], column[k - 1]) for k in range(1, depth)
        ]

    def finish(acc, landed, copies):
        value = acc[row, z].astype(f32)
        for k in range(1, depth):
            copies[k - 1].wait_recv()
            value = value + landed[k - 1].astype(f32)
        return value

    def swap(source, target):
        return [
            post(source.at[level(k)], target.at[z], column[k - 1]) for k in range(1, depth)
        ]

    def hand_out(source, target):
        out = []
        for k in range(depth):
            for flip in range(2):
                if k or flip:
                    to = core if flip == 0 else 1 - core
                    piece = pl.ds(pl.multiple_of((2 * level(k) + to) * span, ROWS), span)
                    out.append(
                        post(
                            source.at[:, piece, :],
                            target.at[z, own_heads],
                            place(y, x, level(k), to),
                        )
                    )
        return out

    acc_a[...] = parts_a[...]
    hop_a = first_hop(acc_a, in_a1)
    moved = swap(result_own, result) + swap(input_own, input_grad)
    moved += hand_out(final_half, final_out) + hand_out(start_half, start_out)
    sib_b.wait_recv()
    for at_row in range(4):
        acc_b[at_row] = (
            parts_b[at_row, :, core].astype(f32) + from_sib[at_row].astype(f32)
        ).astype(bf)
    hop_b = first_hop(acc_b, in_b1)
    sib_s.wait_recv()
    total[1] = total[0] + in_s[0]
    sum_x = post(total.at[1], in_s.at[1], beside_x)
    hop_a = second_hop(acc_a, in_a1, in_a2, hop_a)
    sum_x.wait_recv()
    total[2] = total[1] + in_s[1]
    sum_y = post(total.at[2], in_s.at[2], beside_y)
    hop_a = third_hop(acc_a, in_a2, in_a3, hop_a)
    sum_y.wait_recv()
    total[3] = total[2] + in_s[2]
    sum_z = [post(total.at[3], in_s.at[2 + k], column[k - 1]) for k in range(1, depth)]
    hop_b = second_hop(acc_b, in_b1, in_b2, hop_b)
    hop_b = third_hop(acc_b, in_b2, in_b3, hop_b)
    last_a[0] = finish(acc_a, in_a3, hop_a)
    swap_a = post(last_a.at[0, 1 - core], last_a.at[1, 0], sibling)
    value = total[3]
    for k in range(1, depth):
        sum_z[k - 1].wait_recv()
        value = value + in_s[2 + k]
    sums[...] = value
    value = finish(acc_b, in_b3, hop_b)
    model = grad_out.shape[1]
    groups = grad_up.shape[1] // model
    grad_out[...] = value[0:ROWS]
    for group in range(groups):
        grad_up[:, group * model : (group + 1) * model] = value[
            ROWS * (group + 1) : ROWS * (group + 2)
        ]
    grad_down[...] = value[ROWS * (groups + 1) :]
    swap_a.wait_recv()
    width = model // 2
    for source, part in ((last_a[0, core], core), (last_a[1, 0], 1 - core)):
        lanes = pl.ds(pl.multiple_of(part * width, LANES), width)
        grad_q[:, lanes] = source[:, :width]
        grad_k[:, lanes] = source[:, width : 2 * width]
        grad_v[:, lanes] = source[:, 2 * width : 3 * width]
        grad_gate[:, pl.ds(pl.multiple_of(part * LANES, LANES), LANES)] = source[:, 3 * width :]
    for copy in moved:
        copy.wait_recv()
    post.close()


def vmem(count):
    return [pl.BlockSpec(memory_space=pltpu.VMEM)] * count


def shaped(*dims, dtype=f32):
    return jax.ShapeDtypeStruct(dims, dtype)


def run(kernel, outs, scratch, copies, identity, *args):
    return pl.pallas_call(
        kernel,
        out_shape=outs,
        in_specs=vmem(len(args)),
        out_specs=vmem(len(outs)),
        scratch_shapes=list(scratch) + [pltpu.SemaphoreType.DMA((copies,))] * 2,
        compiler_params=pltpu.CompilerParams(
            collective_id=identity, has_side_effects=True, vmem_limit_bytes=VMEM
        ),
        name=kernel.__name__,
    )(*args)


def fast_body(
    tokens, w_query, w_key, w_value, w_gate, w_out, w_up, w_down,
    gain_one, shift_one, gain_two, shift_two, bias_up, bias_down,
    gate_bias, start_state, start_norm, rand_feat, out_grad, state_grad, norm_grad,
):
    depth, block, model = tokens.shape
    all_heads, feat, head_dim = rand_feat.shape
    heads = all_heads // 2
    width = heads * head_dim
    half = 3 * width + LANES
    seq = lax.axis_index("seq")
    device = lax.axis_index("row") * 2 * depth + seq
    z, core = seq // 2, seq % 2
    groups = w_up.shape[1] // model
    rows_b = ROWS * (groups + 1) + w_down.shape[0]
    chunk = 2 * block
    lane = jnp.arange(model)
    one_hot = (lane // ROWS == device)[None, :]
    vectors = jnp.stack([gain_one, shift_one, gain_two, shift_two, bias_down])
    vectors = jnp.where(one_hot, jnp.tile(vectors, (1, model // ROWS)), 0.0)
    owned = w_down.shape[0]
    place_up = jnp.arange(groups * model).reshape(groups, model) // owned == device
    up_rows = jnp.where(place_up, jnp.tile(bias_up, model // owned)[None, :], 0.0)
    small = jnp.concatenate([vectors, up_rows, jnp.zeros((ROWS - 5 - groups, model), f32)])
    gate_cols = jnp.zeros((ROWS, 2, LANES), f32).at[:, :, :heads].set(w_gate.reshape(ROWS, 2, heads))
    spare = LANES - head_dim - 1

    def widen(state, norm):
        pad = jnp.zeros(norm.shape + (spare,), f32)
        return jnp.concatenate([state, norm[..., None], pad], axis=-1)

    carried = widen(state_grad, norm_grad).astype(bf)
    begin = widen(
        lax.dynamic_slice(start_state, (z, heads * core, 0, 0), (1, heads, feat, head_dim))[0],
        lax.dynamic_slice(start_norm, (z, heads * core, 0), (1, heads, feat))[0],
    )
    own_feat = lax.dynamic_slice_in_dim(rand_feat, heads * core, heads, 0)
    eye = jnp.eye(heads, dtype=bool)[:, None, :, None]
    spread = jnp.where(eye, own_feat[:, :, None, :], 0.0).reshape(heads * feat, width)
    own_bias = jnp.zeros((1, LANES), f32).at[0, :heads].set(
        lax.dynamic_slice_in_dim(gate_bias, heads * core, heads, 0)
    )
    ga, gb, x_own, dy_own, sg = run(
        gather_kernel,
        [
            shaped(4, depth, 2, ROWS, 2 * half + model, dtype=bf),
            shaped(4, depth, 2, rows_b, model, dtype=bf),
            shaped(depth, block, model, dtype=bf),
            shaped(depth, block, model, dtype=bf),
            shaped(2 * depth, heads, feat // (2 * depth), LANES, dtype=bf),
        ],
        [],
        64,
        0,
        w_query, w_key, w_value, w_out, w_up, w_down, gate_cols.reshape(ROWS, 2 * LANES),
        small.astype(bf), tokens, out_grad, carried,
    )
    constants = [
        pltpu.VMEM((width, width), bf),
        pltpu.VMEM((chunk, chunk), bf),
        pltpu.VMEM((heads * feat, width), bf),
        pltpu.VMEM((heads * feat, width), bf),
    ]
    proj, first, attended, states, raw = run(
        mix_kernel,
        [
            shaped(2, depth, block, half),
            shaped(2, depth, block, model, dtype=bf),
            shaped(depth, block, model, dtype=bf),
            shaped(depth + 1, heads, feat, LANES),
            shaped(heads, 2, depth, block, LANES),
        ],
        constants + [pltpu.VMEM((2, depth, block, width), bf)],
        2,
        1,
        ga, x_own, spread, own_bias, begin,
    )
    tall = (depth * block, model)
    result, parts_b, grad_mixed, grad_att, sums = run(
        ff_kernel,
        [
            shaped(depth, block, model, dtype=bf),
            shaped(4, depth, 2, rows_b, model, dtype=bf),
            shaped(depth, block, model),
            shaped(2, depth, block, width),
            shaped(SUMMED, model),
        ],
        [
            pltpu.VMEM(tall, bf),
            pltpu.VMEM(tall, f32),
            pltpu.VMEM(tall, f32),
            pltpu.VMEM((depth, block, model), f32),
        ],
        1,
        2,
        ga, gb, x_own, dy_own, attended,
    )
    input_grad, start_grad, parts_a, sums = run(
        unmix_kernel,
        [
            shaped(depth, block, model, dtype=bf),
            shaped(heads, feat, LANES),
            shaped(4, depth, 2, ROWS, half, dtype=bf),
            shaped(SUMMED, model),
        ],
        constants
        + [
            pltpu.VMEM((2, depth, block, half), bf),
            pltpu.VMEM((2, chunk, heads * feat), f32),
            pltpu.VMEM((depth, block, model), f32),
            pltpu.VMEM((depth, block, model), f32),
        ],
        1,
        3,
        ga, x_own, spread, proj, first, states, raw, grad_att, sg, grad_mixed, sums,
    )
    span = feat // (2 * depth)
    back = depth // 2
    piece_a, piece_b = (2, ROWS, half), (rows_b, model)
    (
        grad_q, grad_k, grad_v, grad_gate, grad_out, grad_up, grad_down,
        sums, result, input_grad, final_out, start_out,
    ) = run(
        scatter_kernel,
        [
            shaped(ROWS, model), shaped(ROWS, model), shaped(ROWS, model),
            shaped(ROWS, 2 * LANES), shaped(ROWS, model), shaped(*w_up.shape), shaped(*w_down.shape),
            shaped(SUMMED, model),
            shaped(depth, block, model, dtype=bf), shaped(depth, block, model, dtype=bf),
            shaped(depth, all_heads, span, LANES, dtype=bf), shaped(depth, all_heads, span, LANES, dtype=bf),
        ],
        [
            pltpu.VMEM((4, depth) + piece_a, bf),
            pltpu.VMEM((4, depth) + piece_b, bf),
            pltpu.VMEM((4, depth) + piece_b, bf),
            pltpu.VMEM((2, back, 2) + piece_a, bf),
            pltpu.VMEM((2, back, 2) + piece_b, bf),
            pltpu.VMEM((2, back) + piece_a, bf),
            pltpu.VMEM((2, back) + piece_b, bf),
            pltpu.VMEM((depth - 1,) + piece_a, bf),
            pltpu.VMEM((depth - 1,) + piece_b, bf),
            pltpu.VMEM((2,) + piece_a, f32),
            pltpu.VMEM((heads, feat, LANES), bf),
            pltpu.VMEM((heads, feat, LANES), bf),
            pltpu.VMEM((4, SUMMED, model), f32),
            pltpu.VMEM((depth + 2, SUMMED, model), f32),
        ],
        64,
        4,
        parts_a, parts_b, sums[None], result, input_grad, states[depth], start_grad,
    )
    own = lax.dynamic_slice_in_dim(sums, device * ROWS, ROWS, 1)
    up_own = lax.dynamic_slice_in_dim(
        sums[5 : 5 + groups].reshape(groups * model), device * owned, owned, 0
    )
    gate_total = jnp.concatenate([sums[9, :heads], sums[10, :heads]])
    gate_own = grad_gate.reshape(ROWS, 2, LANES)[:, :, :heads].reshape(ROWS, all_heads)
    final_out, start_out = final_out.astype(f32), start_out.astype(f32)
    return (
        result,
        final_out[..., :head_dim],
        final_out[..., head_dim],
        input_grad,
        start_out[..., :head_dim],
        start_out[..., head_dim],
        grad_q,
        grad_k,
        grad_v,
        gate_own,
        grad_out,
        grad_up,
        grad_down,
        own[0],
        own[1],
        own[2],
        own[3],
        up_own,
        own[4],
        gate_total,
    )


def solution(mesh):
    placed = (
        P("row", "seq", None),
        P(("row", "seq"), None),
        P(("row", "seq"), None),
        P(("row", "seq"), None),
        P(("row", "seq"), None),
        P(("row", "seq"), None),
        P(("row", "seq"), None),
        P(("row", "seq"), None),
        P(("row", "seq")),
        P(("row", "seq")),
        P(("row", "seq")),
        P(("row", "seq")),
        P(("row", "seq")),
        P(("row", "seq")),
        P(),
        P("row", None, None, None),
        P("row", None, None),
        P(),
        P("row", "seq", None),
        P("row", None, "seq", None),
        P("row", None, "seq"),
    )

    def chosen(tokens, *rest):
        whole = mesh.shape["row"] == 4 and 2 * tokens.shape[0] == mesh.shape["seq"]
        return (fast_body if whole else body)(tokens, *rest)

    return jax.shard_map(
        chosen,
        mesh=mesh,
        in_specs=placed,
        out_specs=(
            P("row", "seq", None),
            P("row", None, "seq", None),
            P("row", None, "seq"),
            P("row", "seq", None),
            P("row", None, "seq", None),
            P("row", None, "seq"),
            P(("row", "seq"), None),
            P(("row", "seq"), None),
            P(("row", "seq"), None),
            P(("row", "seq"), None),
            P(("row", "seq"), None),
            P(("row", "seq"), None),
            P(("row", "seq"), None),
            P(("row", "seq")),
            P(("row", "seq")),
            P(("row", "seq")),
            P(("row", "seq")),
            P(("row", "seq")),
            P(("row", "seq")),
            P(),
        ),
        check_vma=False,
    )
```
